32 devices in a mesh: row: 4 (over y, core), col: 8 (over z, x).
Axes of the slice: x: 2, y: 2, z: 4, core: 2. Of those that a mesh axis runs over, the one named last changes fastest.
Arguments:
- chol_window: bfloat16 [48, 48, 1536], P(None, None, ('row', 'col')), may hold values from -0.3125 to 0.3125
- chol_pairs: bfloat16 [512, 512, 1536], P('row', 'col'), may hold values from -0.3125 to 0.3125
- amplitudes: bfloat16 [48, 512, 1024], P(None, 'col', 'row'), may hold values from -6 to 6
- eps_window: float32 [48], P('col'), may hold values from 0.5 to 2
- eps_virtual: float32 [512], P('row'), may hold values from 0.5 to 2
- eps_occupied: float32 [1024], replicated, may hold values from 0.5 to 2
- dress_first: bfloat16 [1024, 1024], replicated, may hold values from -0.1875 to 0.1875
- dress_second: bfloat16 [1024, 1024], replicated, may hold values from -0.1875 to 0.1875
Outputs:
- resid: bfloat16 [48, 512, 1024], P('col', None, 'row')
The draws below stay inside these ranges and needn't reach their ends.
All inputs are finite; a program needn't handle non-finite values.
Results may differ from the reference program's by a relative error of at most 0.0061.
Values may be sent and summed in bfloat16 or wider, within the bound.
A program may use at most 192 MiB of HBM per device.

```python
import math
import jax
import jax.numpy as jnp
from jax import lax

VIRT = 512
NAUX = 1536
OCC = 1024
VW = 48


def shard_levels(stream_key, shape, pieces, least, largest):
    loudness = 1.0
    for dim, blocks in pieces:
        heights = jax.random.uniform(jax.random.fold_in(jax.random.fold_in(stream_key, 6), dim), (blocks,), jnp.float32, least / len(pieces), largest / len(pieces))
        loudness = loudness * jnp.repeat(jnp.exp(heights), shape[dim] // blocks).reshape((-1,) + (1,) * (len(shape) - 1 - dim))
    return loudness


def normal_values(rng, shape, scale, limit, split=(), dtype=jnp.bfloat16):
    result = jax.random.normal(rng, shape, jnp.float32) * scale
    if len(split) > 0:
        result = shard_levels(rng, shape, split, -0.22, 0.18) * result
    return jnp.clip(result, min=-limit, max=limit).astype(dtype)


def setup_inputs(seed: int = 0) -> dict:
    arg_keys = jax.random.split(jax.random.key(seed), 9)
    return {
        "chol_window": normal_values(arg_keys[0], (VW, VW, NAUX), ((3.0 / (VW * VIRT * NAUX) ** 0.5) ** 0.5), 0.3125, ((2, 32),)),
        "chol_pairs": normal_values(arg_keys[1], (VIRT, VIRT, NAUX), ((3.0 / (VW * VIRT * NAUX) ** 0.5) ** 0.5), 0.3125, ((0, 4), (1, 8))),
        "amplitudes": normal_values(arg_keys[2], (VW, VIRT, OCC), 1.0, 6.0, ((1, 8), (2, 4))),
        "eps_window": jnp.clip(jnp.exp(math.log(2.0) - 1.3862944 * jax.random.uniform(arg_keys[3], (VW,), jnp.float32) ** shard_levels(arg_keys[3], (VW,), ((0, 8),), -0.2, 0.2)), 0.5, 2.0),
        "eps_virtual": jnp.clip(jnp.exp(math.log(2.0) - 1.3862944 * jax.random.uniform(arg_keys[4], (VIRT,), jnp.float32) ** shard_levels(arg_keys[4], (VIRT,), ((0, 4),), -0.2, 0.2)), 0.5, 2.0),
        "eps_occupied": jnp.clip(jnp.exp(jax.random.uniform(arg_keys[5], (OCC,), jnp.float32, math.log(0.5), math.log(2.0))), 0.5, 2.0),
        "dress_first": normal_values(arg_keys[6], (OCC, OCC), OCC ** -0.5, 0.1875),
        "dress_second": normal_values(arg_keys[7], (OCC, OCC), OCC ** -0.5, 0.1875),
    }


def reference(chol_window, chol_pairs, amplitudes, eps_window, eps_virtual, eps_occupied, dress_first, dress_second):
    window_f32 = chol_window.astype(jnp.float32)
    pairs_f32 = chol_pairs.astype(jnp.float32)
    amp_f32 = amplitudes.astype(jnp.float32)

    def per_virtual(aux_row):
        tile = jnp.einsum("cq,bdq->bcd", aux_row, pairs_f32).astype(jnp.bfloat16)
        tile = lax.optimization_barrier(tile).astype(jnp.float32)
        return jnp.einsum("bcd,cdo->bo", tile, amp_f32)

    ladder = lax.map(per_virtual, window_f32)
    denominator = eps_window[:, None, None] + eps_virtual[None, :, None] + eps_occupied[None, None, :]
    scaled = (ladder / denominator).astype(jnp.bfloat16)
    flattened = scaled.reshape(VW * VIRT, OCC)
    first_mix = jnp.dot(flattened, dress_first, preferred_element_type=jnp.float32).astype(jnp.bfloat16)
    mixed = flattened.astype(jnp.float32) + jnp.dot(first_mix, dress_second, preferred_element_type=jnp.float32)
    return mixed.astype(jnp.bfloat16).reshape(VW, VIRT, OCC)
```

```python
import functools

import jax
import jax.numpy as jnp
from jax import lax
from jax.experimental import pallas as pl
from jax.experimental.pallas import tpu as pltpu
from jax.sharding import PartitionSpec as P

F32 = jnp.float32
BF16 = jnp.bfloat16


def ladder_kernel(rows, win, block_b, window_ref, pairs_ref, amps_ref, out_ref, mixed):
    step = pl.program_id(0)
    count = pairs_ref.shape[0] // block_b
    pair = 2 if count % 2 == 0 else 1

    def body(index, carry):
        start = pl.multiple_of(index * (pair * block_b), pair * block_b)
        tile = pairs_ref[pl.ds(start, pair * block_b), :]
        values = lax.dot_general(
            window_ref[...], tile, (((1,), (1,)), ((), ())), preferred_element_type=F32
        ).astype(BF16)
        for k in range(pair):
            at = pl.multiple_of((step * count + index * pair + k) * win, win)
            for a in range(rows):
                mixed[pl.ds(at, win), a * block_b : (a + 1) * block_b] = values[
                    a * win : (a + 1) * win, k * block_b : (k + 1) * block_b
                ]
        return carry

    lax.fori_loop(0, count // pair, body, 0)

    @pl.when(step == pl.num_programs(0) - 1)
    def _():
        width = 256

        def contract(index, carry):
            at = pl.multiple_of(index * width, width)
            out_ref[:, pl.ds(at, width)] = jnp.dot(
                amps_ref[...], mixed[:, pl.ds(at, width)], preferred_element_type=F32
            ).astype(BF16)
            return carry

        lax.fori_loop(0, out_ref.shape[1] // width, contract, 0)


def ladder_part(window, pairs, amps, rows, block_b):
    win = window.shape[0] // rows
    depth = pairs.shape[1]
    block_d = pairs.shape[0] // block_b
    occ = amps.shape[0]
    if block_b % 128 or win % 16 or (rows * block_b) % 256 or block_d % 8:
        values = jnp.einsum(
            "acq,dbq->dcab",
            window.reshape(rows, win, depth),
            pairs.reshape(block_d, block_b, depth),
            preferred_element_type=F32,
        ).astype(BF16)
        values = values.reshape(block_d * win, rows * block_b)
        return jnp.dot(amps, values, preferred_element_type=F32).astype(BF16)
    group = 8 * block_b
    total = block_d * win
    return pl.pallas_call(
        functools.partial(ladder_kernel, rows, win, block_b),
        out_shape=jax.ShapeDtypeStruct((occ, rows * block_b), BF16),
        grid=(pairs.shape[0] // group,),
        in_specs=[
            pl.BlockSpec(window.shape, lambda i: (0, 0)),
            pl.BlockSpec((group, depth), lambda i: (i, 0)),
            pl.BlockSpec(amps.shape, lambda i: (0, 0)),
        ],
        out_specs=pl.BlockSpec((occ, rows * block_b), lambda i: (0, 0)),
        scratch_shapes=[pltpu.VMEM((total, rows * block_b), BF16)],
        compiler_params=pltpu.CompilerParams(
            dimension_semantics=("arbitrary",), vmem_limit_bytes=48 * 1024 * 1024
        ),
        cost_estimate=pl.CostEstimate(
            flops=2 * rows * block_b * total * (depth + occ),
            bytes_accessed=2 * (pairs.size + amps.size + window.size + occ * rows * block_b),
            transcendentals=0,
        ),
    )(window, pairs, amps)


def add(left, right):
    return left.astype(F32) + right.astype(F32)


def local(
    cols,
    chol_window,
    chol_pairs,
    amplitudes,
    eps_window,
    eps_virtual,
    eps_occupied,
    dress_first,
    dress_second,
):
    win = chol_window.shape[0]
    block_b, block_d, depth = chol_pairs.shape
    rows = win // cols
    occ = eps_occupied.shape[0]

    inner = 1 << ((cols.bit_length() - 1) // 2)
    outer = cols // inner
    me = lax.axis_index("col")
    my_outer, my_inner = me // inner, lax.rem(me, inner)
    next_inner = [(o * inner + i, o * inner + (i + 1) % inner) for o in range(outer) for i in range(inner)]
    next_outer = [(o * inner + i, ((o + 1) % outer) * inner + i) for o in range(outer) for i in range(inner)]

    window = chol_window.reshape(win * win, -1).T
    window = lax.all_gather(window, "col", axis=0, tiled=True)
    window = lax.all_gather(window, "row", axis=0, tiled=True)
    window = window.T
    amps = amplitudes.transpose(2, 1, 0).reshape(amplitudes.shape[2], block_d * win)
    amps = lax.all_gather(amps, "row", axis=0, tiled=True)
    pairs = chol_pairs.transpose(1, 0, 2).reshape(block_d * block_b, depth)

    def part(to_outer, to_inner):
        target = to_outer * inner + to_inner
        piece = lax.dynamic_slice_in_dim(window, target * (rows * win), rows * win, 0)
        return ladder_part(piece, pairs, amps, rows, block_b)

    moving = None
    for hop in range(outer):
        to_outer = lax.rem(my_outer + (2 * outer - 1 - hop), outer)
        held = None
        for step in range(inner):
            to_inner = lax.rem(my_inner + (2 * inner - 1 - step), inner)
            mine = part(to_outer, to_inner)
            held = mine if held is None else add(held, mine)
            if step < inner - 1:
                held = lax.ppermute(held.astype(BF16), "col", next_inner)
        held = held if moving is None else add(moving, held)
        if hop < outer - 1:
            moving = lax.ppermute(held.astype(BF16), "col", next_outer)

    summed = held.T.reshape(rows, block_b, occ)
    denominator = (
        eps_window[:, None, None] + eps_virtual[None, :, None] + eps_occupied[None, None, :]
    )
    scaled = (summed / denominator).astype(BF16)
    flattened = scaled.reshape(rows * block_b, occ)
    first_mix = jnp.dot(flattened, dress_first, preferred_element_type=F32).astype(BF16)
    mixed = flattened.astype(F32) + jnp.dot(first_mix, dress_second, preferred_element_type=F32)
    mixed = mixed.astype(BF16).reshape(rows, block_b, occ)
    return lax.all_to_all(mixed, "row", split_axis=2, concat_axis=1, tiled=True)


def solution(mesh):
    return jax.shard_map(
        functools.partial(local, mesh.shape["col"]),
        mesh=mesh,
        in_specs=(
            P(None, None, ("row", "col")),
            P("row", "col", None),
            P(None, "col", "row"),
            P("col"),
            P("row"),
            P(),
            P(),
            P(),
        ),
        out_specs=P("col", None, "row"),
        check_vma=False,
    )
```

```python
import functools

import jax
import jax.numpy as jnp
from jax import lax
from jax.experimental import pallas as pl
from jax.experimental.layout import Layout, with_layout_constraint
from jax.experimental.pallas import tpu as pltpu
from jax.sharding import PartitionSpec as P

F32 = jnp.float32
BF16 = jnp.bfloat16


def ladder_kernel(rows, win, block_b, parts, window_ref, pairs_ref, amps_hbm, *rest):
    out_refs, (mixed, amps, sem) = rest[:parts], rest[parts:]
    step = pl.program_id(0)
    count = pairs_ref.shape[0] // block_b
    pair = 2
    load = pltpu.make_async_copy(amps_hbm, amps, sem)

    @pl.when(step == 0)
    def _():
        load.start()

    def body(index, carry):
        start = pl.multiple_of(index * (pair * block_b), pair * block_b)
        tile = pairs_ref[pl.ds(start, pair * block_b), :]
        values = lax.dot_general(
            window_ref[...], tile, (((1,), (1,)), ((), ())), preferred_element_type=F32
        ).astype(BF16)
        for k in range(pair):
            at = pl.multiple_of((step * count + index * pair + k) * win, win)
            for a in range(parts * rows):
                mixed[pl.ds(at, win), a * block_b : (a + 1) * block_b] = values[
                    a * win : (a + 1) * win, k * block_b : (k + 1) * block_b
                ]
        return carry

    lax.fori_loop(0, count // pair, body, 0)

    @pl.when(step == pl.num_programs(0) - 1)
    def _():
        load.wait()
        width = 256
        for k in range(parts):
            out_ref = out_refs[k]

            def contract(index, carry):
                at = pl.multiple_of(index * width, width)
                source = pl.multiple_of(k * rows * block_b + index * width, width)
                out_ref[:, pl.ds(at, width)] = jnp.dot(
                    amps[...], mixed[:, pl.ds(source, width)], preferred_element_type=F32
                ).astype(BF16)
                return carry

            lax.fori_loop(0, rows * block_b // width, contract, 0)


def ladder_part(window, pairs, amps, rows, win, block_b):
    parts = window.shape[0] // (rows * win)
    depth = pairs.shape[1]
    block_d = pairs.shape[0] // block_b
    occ = amps.shape[0]
    if block_b % 128 or win % 16 or (rows * block_b) % 256 or block_d % 8:
        values = jnp.einsum(
            "pacq,dbq->pdcab",
            window.reshape(parts, rows, win, depth),
            pairs.reshape(block_d, block_b, depth),
            preferred_element_type=F32,
        ).astype(BF16)
        values = values.reshape(parts, block_d * win, rows * block_b)
        return [jnp.dot(amps, v, preferred_element_type=F32).astype(BF16) for v in values]
    group = 8 * block_b
    total = block_d * win
    width = rows * block_b
    return pl.pallas_call(
        functools.partial(ladder_kernel, rows, win, block_b, parts),
        out_shape=[jax.ShapeDtypeStruct((occ, width), BF16)] * parts,
        grid=(pairs.shape[0] // group,),
        in_specs=[
            pl.BlockSpec(window.shape, lambda i: (0, 0)),
            pl.BlockSpec((group, depth), lambda i: (i, 0)),
            pl.BlockSpec(memory_space=pl.ANY),
        ],
        out_specs=[pl.BlockSpec((occ, width), lambda i: (0, 0))] * parts,
        scratch_shapes=[
            pltpu.VMEM((total, parts * width), BF16),
            pltpu.VMEM(amps.shape, BF16),
            pltpu.SemaphoreType.DMA,
        ],
        compiler_params=pltpu.CompilerParams(
            dimension_semantics=("arbitrary",), vmem_limit_bytes=48 * 1024 * 1024
        ),
        cost_estimate=pl.CostEstimate(
            flops=2 * parts * width * total * (depth + occ),
            bytes_accessed=2 * (pairs.size + amps.size + window.size + parts * occ * width),
            transcendentals=0,
        ),
    )(window, pairs, amps)


def row_major(array):
    return with_layout_constraint(array, Layout(tuple(range(array.ndim))))


def gather_ring(block, name, ring, size, place):
    stack = jnp.zeros((size,) + block.shape, block.dtype)
    stack = lax.dynamic_update_index_in_dim(stack, block, place, 0)
    for step in range(1, size):
        block = lax.ppermute(block, name, ring)
        stack = lax.dynamic_update_index_in_dim(stack, block, lax.rem(place + size - step, size), 0)
    return stack


def add(left, right):
    return left.astype(F32) + right.astype(F32)


def local(
    row_count,
    cols,
    chol_window,
    chol_pairs,
    amplitudes,
    eps_window,
    eps_virtual,
    eps_occupied,
    dress_first,
    dress_second,
):
    win = chol_window.shape[0]
    block_b, block_d, depth = chol_pairs.shape
    rows = win // cols
    occ = eps_occupied.shape[0]

    inner = 1 << ((cols.bit_length() - 1) // 2)
    outer = cols // inner
    me = lax.axis_index("col")
    my_outer, my_inner = me // inner, lax.rem(me, inner)
    next_inner = [(o * inner + i, o * inner + (i + 1) % inner) for o in range(outer) for i in range(inner)]
    next_outer = [(o * inner + i, ((o + 1) % outer) * inner + i) for o in range(outer) for i in range(inner)]

    cores = 2 if row_count % 2 == 0 else 1
    ys = row_count // cores
    my_row = lax.axis_index("row")
    my_y, my_core = my_row // cores, lax.rem(my_row, cores)
    next_y = [(r, (r + cores) % row_count) for r in range(row_count)]
    next_core = [(y * cores + c, y * cores + (c + 1) % cores) for y in range(ys) for c in range(cores)]
    over_x = lambda block: gather_ring(block, "col", next_inner, inner, my_inner)
    over_z = lambda block: gather_ring(block, "col", next_outer, outer, my_outer)
    over_y = lambda block: gather_ring(block, "row", next_y, ys, my_y)
    over_core = lambda block: gather_ring(block, "row", next_core, cores, my_core)

    amps = amplitudes.transpose(2, 1, 0).reshape(amplitudes.shape[2], block_d * win)
    amps = row_major(amps)
    amps = over_core(over_y(amps)).transpose(1, 0, 2, 3).reshape(occ, block_d * win)

    slices = chol_window.reshape(win * win, -1).T
    half = win * win // 2
    one, two = slices[:, :half], slices[:, half:]
    one = over_z(over_x(one))
    two = over_z(over_y(two))
    one, two, chol_pairs = lax.optimization_barrier((one, two, chol_pairs))
    one = row_major(one.reshape(-1, half).T)
    one = over_core(over_y(one))
    two = over_x(two)
    two = row_major(two.transpose(2, 4, 1, 0, 3).reshape(ys, half, -1))
    two = over_core(two)
    window = jnp.concatenate(
        [
            jnp.concatenate([one[c, y], two[c, y]], axis=0)
            for y in range(ys)
            for c in range(cores)
        ],
        axis=1,
    )
    pairs = chol_pairs.transpose(1, 0, 2).reshape(block_d * block_b, depth)

    def parts_for(to_outer, to_inners):
        pieces = [
            lax.dynamic_slice_in_dim(window, (to_outer * inner + i) * (rows * win), rows * win, 0)
            for i in to_inners
        ]
        return ladder_part(jnp.concatenate(pieces, axis=0), pairs, amps, rows, win, block_b)

    to_inners = [lax.rem(my_inner + (2 * inner - 1 - step), inner) for step in range(inner)]
    moving = None
    for hop in range(outer):
        to_outer = lax.rem(my_outer + (2 * outer - 1 - hop), outer)
        held = None
        if hop < outer - 1:
            parts = parts_for(to_outer, to_inners)
        else:
            parts = [parts_for(to_outer, [i])[0] for i in to_inners]
        for step, mine in enumerate(parts):
            held = mine if held is None else add(held, mine)
            if step < inner - 1:
                held = lax.ppermute(held.astype(BF16), "col", next_inner)
        held = held if moving is None else add(moving, held)
        if hop < outer - 1:
            moving = lax.ppermute(held.astype(BF16), "col", next_outer)

    summed = held.T.reshape(rows, block_b, occ)
    denominator = (
        eps_window[:, None, None] + eps_virtual[None, :, None] + eps_occupied[None, None, :]
    )
    scaled = (summed / denominator).astype(BF16)
    flattened = scaled.reshape(rows * block_b, occ)
    first_mix = jnp.dot(flattened, dress_first, preferred_element_type=F32).astype(BF16)
    width = occ // row_count
    out = jnp.zeros((rows, row_count * block_b, width), BF16)
    for shift in [*range(1, row_count), 0]:
        start = lax.rem(my_row + shift, row_count) * width
        block = lax.dynamic_slice_in_dim(flattened, start, width, 1).astype(F32)
        columns = lax.dynamic_slice_in_dim(dress_second, start, width, 1)
        block = (block + jnp.dot(first_mix, columns, preferred_element_type=F32)).astype(BF16)
        if shift:
            block = lax.ppermute(block, "row", [(r, (r + shift) % row_count) for r in range(row_count)])
        source = lax.rem(my_row + row_count - shift, row_count) * block_b
        out = lax.dynamic_update_slice_in_dim(out, block.reshape(rows, block_b, width), source, 1)
    return out


def solution(mesh):
    return jax.shard_map(
        functools.partial(local, mesh.shape["row"], mesh.shape["col"]),
        mesh=mesh,
        in_specs=(
            P(None, None, ("row", "col")),
            P("row", "col", None),
            P(None, "col", "row"),
            P("col"),
            P("row"),
            P(),
            P(),
            P(),
        ),
        out_specs=P("col", None, "row"),
        check_vma=False,
    )
```
